32 devices in a mesh: ctx: 16 (over z, y, core), head: 2 (over x).
Axes of the slice: x: 2, y: 2, z: 4, core: 2. Of those that a mesh axis runs over, the one named last changes fastest.
Arguments:
- queries: bfloat16 [32768, 2048], P('ctx', 'head'), may hold values from -6 to 6
- key_vectors: bfloat16 [32768, 2048], P('ctx', 'head'), may hold values from -6 to 6
- values: bfloat16 [32768, 2048], P('ctx', 'head'), may hold values from -6 to 6
- out_grad: bfloat16 [32768, 2048], P('ctx', 'head'), may hold values from -6 to 6
- level_logits: float32 [16, 5, 32768], P('head', None, 'ctx'), may hold values from -6 to 6
- level_proj: bfloat16 [80, 2048], P(None, 'head'), may hold values from -0.3125 to 0.3125
Outputs:
- grad_queries: bfloat16 [32768, 2048], P('ctx', 'head')
- grad_keys: bfloat16 [32768, 2048], P('ctx', 'head')
- grad_values: bfloat16 [32768, 2048], P('ctx', 'head')
- level_grad: float32 [16, 5, 32768], P('head', None, 'ctx')
- hidden_grad: bfloat16 [32768, 2048], P('ctx', 'head')
The draws below stay inside these ranges and needn't reach their ends.
All inputs are finite; a program needn't handle non-finite values.
Results may differ from the reference program's by a relative error of at most 0.0058.
Values may be sent and summed in bfloat16 or wider, within the bound.
A program may use at most 384 MiB of HBM per device.

```python
import jax
import jax.numpy as jnp
from jax import lax

TOK_DEV = 2048
HEADS = 16
DK = 128
LEVELS = 5
TOKENS = 32768


def block_scale(own_key, extent, split, low, high):
    factor_of = 1.0
    for dim, parts in split:
        heights = jax.random.uniform(jax.random.fold_in(jax.random.fold_in(own_key, 6), dim), (parts,), jnp.float32, low / len(split), high / len(split))
        factor_of = factor_of * jnp.repeat(jnp.exp(heights), extent[dim] // parts).reshape((-1,) + (1,) * (len(extent) - 1 - dim))
    return factor_of


def centred(rng, shape, scale, bound, pieces=(), kind=jnp.bfloat16):
    drawn = jax.random.normal(rng, shape, jnp.float32) * scale
    if len(pieces) > 0:
        drawn = block_scale(rng, shape, pieces, -0.22, 0.18) * drawn
    return jnp.clip(drawn, min=-bound, max=bound).astype(kind)


def setup_inputs(seed: int = 0) -> dict:
    key_of = jax.random.split(jax.random.key(seed), 7)
    return {
        "queries": centred(key_of[0], (TOKENS, HEADS * DK), 1.0, 6.0, ((0, 16), (1, 2))),
        "key_vectors": centred(key_of[1], (TOKENS, HEADS * DK), 1.0, 6.0, ((0, 16), (1, 2))),
        "values": centred(key_of[2], (TOKENS, HEADS * DK), 1.0, 6.0, ((0, 16), (1, 2))),
        "out_grad": centred(key_of[3], (TOKENS, HEADS * DK), 1.0, 6.0, ((0, 16), (1, 2))),
        "level_logits": centred(key_of[4], (HEADS, LEVELS, TOKENS), 1.5, 6.0, ((0, 2), (2, 16)), jnp.float32),
        "level_proj": centred(key_of[5], (HEADS * LEVELS, HEADS * DK), (4 * HEADS * LEVELS) ** -0.5, 0.3125, ((1, 2),)),
    }


HIGHEST = lax.Precision.HIGHEST


def round_bf(array):
    return lax.optimization_barrier(array.astype(jnp.bfloat16)).astype(jnp.float32)


def reference(queries, key_vectors, values, out_grad, level_logits, level_proj):
    group_count = TOKENS // TOK_DEV
    scaling = float(DK * TOKENS) ** -0.5
    f32 = jnp.float32

    def split_heads(array):
        return array.reshape(group_count, TOK_DEV, HEADS, DK)

    query_c = split_heads(queries)
    key_c = split_heads(key_vectors)
    value_c = split_heads(values)
    cotan_c = split_heads(out_grad)
    gates = jax.nn.softplus(level_logits)
    gates_c = gates.reshape(HEADS, LEVELS, group_count, TOK_DEV).transpose(2, 1, 3, 0)
    causal = jnp.arange(TOK_DEV)[None, :] <= jnp.arange(TOK_DEV)[:, None]

    def group_local(operands):
        query_blk, key_blk, value_blk, cotan_blk, gate_zero = operands
        query_f = query_blk.astype(f32)
        key_f = key_blk.astype(f32)
        value_f = value_blk.astype(f32)
        cotan_f = cotan_blk.astype(f32)
        scores = jnp.einsum("qhd,khd->hqk", query_f, key_f, precision=HIGHEST)
        products = jnp.einsum("qhd,khd->hqk", cotan_f, value_f, precision=HIGHEST)
        weight = jnp.where(causal[None], scaling * gate_zero.T[:, :, None], 0.0)
        prod_weighted = round_bf(weight * products)
        score_weighted = round_bf(weight * scores)
        grad_query = jnp.einsum("hqk,khd->qhd", prod_weighted, key_f, precision=HIGHEST)
        grad_key = jnp.einsum("hqk,qhd->khd", prod_weighted, query_f, precision=HIGHEST)
        grad_value = jnp.einsum("hqk,qhd->khd", score_weighted, cotan_f, precision=HIGHEST)
        gate_grad = scaling * jnp.sum(jnp.where(causal[None], scores * products, 0.0), axis=2)
        return grad_query, grad_key, grad_value, gate_grad

    local_q, local_k, local_v, gate_zero_grad = lax.map(group_local, (query_c, key_c, value_c, cotan_c, gates_c[:, 0]))

    query_f = query_c.astype(f32)
    key_f = key_c.astype(f32)
    value_f = value_c.astype(f32)
    cotan_f = cotan_c.astype(f32)
    group_state = jnp.einsum("nchd,nche->nhde", key_f, value_f, precision=HIGHEST)
    group_ids = jnp.arange(group_count, dtype=jnp.int32)
    grad_q = local_q
    adjoint_state = jnp.zeros_like(group_state)
    level_terms = [gate_zero_grad.transpose(0, 2, 1)]
    for level_idx in range(1, LEVELS):
        span = 2 ** (level_idx - 1)
        is_upper = jnp.bitwise_and(jnp.right_shift(group_ids, level_idx - 1), 1).astype(f32)[:, None, None, None]
        block_sums = group_state.reshape(group_count // span, span, HEADS, DK, DK).sum(axis=1)
        before = jnp.concatenate([jnp.zeros_like(block_sums[:1]), block_sums[:-1]], axis=0)
        level_state = round_bf(jnp.repeat(before, span, axis=0) * is_upper)
        weights = scaling * gates_c[:, level_idx]
        mapped = jnp.einsum("nche,nhde->nchd", cotan_f, level_state, precision=HIGHEST)
        grad_q = grad_q + weights[..., None] * mapped
        reached = jnp.einsum("nchd,nhde->nche", query_f, level_state, precision=HIGHEST)
        level_terms.append(scaling * jnp.sum(reached * cotan_f, axis=3))
        weighted = round_bf(weights[..., None] * query_f)
        adjoint = jnp.einsum("nchd,nche->nhde", weighted, cotan_f, precision=HIGHEST) * is_upper
        adjoint_blocks = adjoint.reshape(group_count // span, span, HEADS, DK, DK).sum(axis=1)
        after = jnp.concatenate([adjoint_blocks[1:], jnp.zeros_like(adjoint_blocks[:1])], axis=0)
        adjoint_state = adjoint_state + jnp.repeat(after, span, axis=0) * (1.0 - is_upper)
    adjoint_round = round_bf(adjoint_state)
    grad_k = local_k + jnp.einsum("nche,nhde->nchd", value_f, adjoint_round, precision=HIGHEST)
    grad_v = local_v + jnp.einsum("nchd,nhde->nche", key_f, adjoint_round, precision=HIGHEST)
    stacked = jnp.stack(level_terms, axis=1).transpose(3, 1, 0, 2).reshape(HEADS, LEVELS, TOKENS)
    level_grad = stacked * jax.nn.sigmoid(level_logits)
    logit_cot = level_grad.astype(jnp.bfloat16).reshape(HEADS * LEVELS, TOKENS)
    hidden_grad = jnp.dot(logit_cot.T, level_proj, preferred_element_type=jnp.float32)
    width = HEADS * DK
    return (grad_q.reshape(TOKENS, width).astype(jnp.bfloat16),
            grad_k.reshape(TOKENS, width).astype(jnp.bfloat16),
            grad_v.reshape(TOKENS, width).astype(jnp.bfloat16),
            level_grad,
            hidden_grad.astype(jnp.bfloat16))
```

```python
import functools

import jax
import jax.numpy as jnp
from jax import lax
from jax.experimental import pallas as pl
from jax.experimental.pallas import tpu as pltpu
from jax.sharding import PartitionSpec as P

F32 = jnp.float32
BF16 = jnp.bfloat16
VMEM_LIMIT = 56 * 1024 * 1024


def dot(lhs, rhs, contract=((1,), (0,))):
    return lax.dot_general(lhs, rhs, (contract, ((), ())), preferred_element_type=F32)


def softplus(x):
    return jnp.maximum(x, 0.0) + jnp.log1p(jnp.exp(-jnp.abs(x)))


def states_kernel(scaling, chunk, q_ref, k_ref, v_ref, d_ref, logit_ref, sloc_ref, dloc_ref, g_ref, ds_ref):
    rows, dk = q_ref.shape
    levels = logit_ref.shape[1]
    weights = scaling * softplus(logit_ref[0])
    state = jnp.zeros((dk, dk), F32)
    outer = jnp.zeros(((levels - 1) * dk, dk), F32)
    own = []
    for j in range(rows // chunk):
        part = slice(j * chunk, (j + 1) * chunk)
        k_t = k_ref[part, :].T
        q_t = q_ref[part, :].T.astype(F32)
        sloc_ref[0, j] = state.astype(BF16)
        state = state + dot(k_t, v_ref[part, :])
        weighted = jnp.concatenate(
            [(weights[l : l + 1, part] * q_t).astype(BF16) for l in range(levels)], axis=0
        )
        adjoint = dot(weighted, d_ref[part, :])
        own.append(adjoint[:dk])
        outer = outer + adjoint[dk:]
    g_ref[0] = state
    for l in range(levels - 1):
        ds_ref[l, 0] = outer[l * dk : (l + 1) * dk]
    after = jnp.zeros((dk, dk), F32)
    for j in reversed(range(rows // chunk)):
        dloc_ref[0, j] = after.astype(BF16)
        after = after + own[j]


def grads_kernel(
    scaling, chunk, q_ref, k_ref, v_ref, d_ref, logit_ref, sloc_ref, dloc_ref, s_ref, dg_ref,
    gq_ref, gk_ref, gv_ref, lg_ref, cot_ref,
):
    rows, dk = q_ref.shape
    levels = logit_ref.shape[1]
    logits = logit_ref[0]
    gates = softplus(logits)
    weights = scaling * gates
    gate_slope = jax.nn.sigmoid(logits)
    slope = [gate_slope[l : l + 1] * (scaling if l else 1.0 / gates[0:1]) for l in range(levels)]
    outer_states = jnp.concatenate([s_ref[l, 0] for l in range(levels - 1)], axis=0)
    causal = lax.broadcasted_iota(jnp.int32, (chunk, chunk), 0) <= lax.broadcasted_iota(
        jnp.int32, (chunk, chunk), 1
    )
    for j in range(rows // chunk):
        part = slice(j * chunk, (j + 1) * chunk)
        q, k, v, d = q_ref[part, :], k_ref[part, :], v_ref[part, :], d_ref[part, :]
        q_t, k_t, d_t = q.T, k.T, d.T
        w0 = weights[0:1, part]
        spread = jnp.where(causal, w0, 0.0)
        score_w = (spread * dot(k, q_t)).astype(BF16)
        prod_w = (spread * dot(v, d_t)).astype(BF16)
        q_f = q_t.astype(F32)
        total = dot(k_t, prod_w) + w0 * dot(sloc_ref[0, j], d_t)
        terms = [jnp.sum(q_f * total, axis=0, keepdims=True) * slope[0][:, part]]
        mapped = dot(outer_states, d_t)
        for l in range(1, levels):
            own = mapped[(l - 1) * dk : l * dk]
            total = total + weights[l : l + 1, part] * own
            terms.append(jnp.sum(q_f * own, axis=0, keepdims=True) * slope[l][:, part])
        level_grad = jnp.concatenate(terms, axis=0)
        lg_ref[0, :, part] = level_grad
        cot_ref[0, :, part] = level_grad.astype(BF16)
        gq_ref[part, :] = total.astype(BF16).T
        carried = (dloc_ref[0, j].astype(F32) + dg_ref[0]).astype(BF16)
        gk_ref[part, :] = (dot(prod_w, q) + dot(v, carried, ((1,), (1,)))).astype(BF16)
        gv_ref[part, :] = (dot(score_w, d) + dot(k, carried)).astype(BF16)


def exchange_kernel(bits, g_ref, ds_ref, s_ref, dg_ref, *scratch):
    (g_out, g_in, f_out, f_in, c_in, d_out, d_in, d0_out, d0_in, a_out, a_in, t_out, t_in, send_sem, recv_sem) = scratch
    me = lax.axis_index("ctx")
    heads = g_ref.shape[0]
    half = heads // 2
    core = me % 2
    mine, other = pl.ds(core * half, half), pl.ds((1 - core) * half, half)
    peers = [me + (1 << b) - 2 * (1 << b) * ((me // (1 << b)) % 2) for b in range(bits)]
    upper = [((me // (1 << b)) % 2).astype(F32) for b in range(bits)]

    barrier = pltpu.get_barrier_semaphore()
    for peer in peers:
        pl.semaphore_signal(barrier, inc=1, device_id={"ctx": peer}, device_id_type=pl.DeviceIdType.MESH)

    for b in range(1, bits):
        d_out[b - 1] = (upper[b] * ds_ref[b, other]).astype(BF16)
    g_out[...] = g_ref[...].astype(BF16)
    d0_out[...] = (upper[0] * ds_ref[0]).astype(BF16)
    pl.semaphore_wait(barrier, bits)

    copies = []

    def send(src, dst, b):
        i = len(copies)
        copy = pltpu.make_async_remote_copy(
            src_ref=src, dst_ref=dst, send_sem=send_sem.at[i], recv_sem=recv_sem.at[i],
            device_id={"ctx": peers[b]}, device_id_type=pl.DeviceIdType.MESH,
        )
        copy.start()
        copies.append(copy)
        return copy

    d_copy = send(d_out, d_in, 0)
    g_copy = send(g_out, g_in, 0)
    d0_copy = send(d0_out, d0_in, 0)

    carried = jnp.zeros((half,) + g_ref.shape[1:], F32)

    def send_adjoint(b, carried):
        pair = upper[b] * ds_ref[b, mine] + d_in[b - 1].astype(F32)
        a_out[b - 1] = (carried + pair).astype(BF16)
        return send(a_out.at[b - 1], a_in.at[b - 1], b)

    d_copy.wait_recv()
    a_copy = send_adjoint(bits - 1, carried)
    g_copy.wait_recv()
    block = g_ref[mine] + g_in[mine].astype(F32)
    f_out[0] = block.astype(BF16)
    f_copy = send(f_out.at[0], f_in.at[0], 1)
    s_ref[0] = g_in[...] * upper[0].astype(BF16)

    forwards = []

    def forward_step(b, block, f_copy):
        f_copy.wait_recv()
        if b + 1 < bits:
            block = block + f_in[b - 1].astype(F32)
            f_out[b] = block.astype(BF16)
            f_copy = send(f_out.at[b], f_in.at[b], b + 1)
        forwards.append(send(f_in.at[b - 1], c_in.at[b - 1], 0))
        s_ref[b, mine] = f_in[b - 1] * upper[b].astype(BF16)
        return block, f_copy

    def adjoint_step(b, carried, a_copy):
        a_copy.wait_recv()
        carried = carried + a_in[b - 1].astype(F32)
        if b > 1:
            return carried, send_adjoint(b - 1, carried)
        t_out[...] = carried.astype(BF16)
        return carried, send(t_out, t_in, 0)

    for b in range(1, bits):
        if b + 1 < bits:
            block, f_copy = forward_step(b, block, f_copy)
        carried, a_copy = adjoint_step(bits - b, carried, a_copy)
        if b + 1 == bits:
            block, f_copy = forward_step(b, block, f_copy)
    d0_copy.wait_recv()
    dg_ref[mine] = carried + d0_in[mine].astype(F32)
    a_copy.wait_recv()
    dg_ref[other] = t_in[...].astype(F32) + d0_in[other].astype(F32)
    for b in range(1, bits):
        forwards[b - 1].wait_recv()
        s_ref[b, other] = c_in[b - 1] * upper[b].astype(BF16)
    for copy in copies:
        copy.wait_send()


def exchange(state, adjoints):
    heads, dk, _ = state.shape
    bits = adjoints.shape[0]
    half = heads // 2
    whole, parts, one = (heads, dk, dk), (bits - 1, half, dk, dk), (half, dk, dk)
    shapes = [whole, whole, parts, parts, parts, parts, parts, whole, whole, parts, parts, one, one]
    count = 4 + 3 * (bits - 1)
    return pl.pallas_call(
        functools.partial(exchange_kernel, bits),
        in_specs=[pl.BlockSpec(memory_space=pltpu.VMEM)] * 2,
        out_specs=[pl.BlockSpec(memory_space=pltpu.VMEM)] * 2,
        out_shape=[
            jax.ShapeDtypeStruct((bits, heads, dk, dk), BF16),
            jax.ShapeDtypeStruct((heads, dk, dk), F32),
        ],
        scratch_shapes=[pltpu.VMEM(s, BF16) for s in shapes]
        + [pltpu.SemaphoreType.DMA((count,)), pltpu.SemaphoreType.DMA((count,))],
        compiler_params=pltpu.CompilerParams(
            collective_id=0, has_side_effects=True, vmem_limit_bytes=VMEM_LIMIT
        ),
        name="exchange",
    )(state, adjoints)


def body(queries, key_vectors, values, out_grad, level_logits, level_proj):
    rows, width = queries.shape
    heads, levels, _ = level_logits.shape
    dk = width // heads
    scaling = float(dk * rows * lax.axis_size("ctx")) ** (-0.5)
    chunk = min(256, rows)
    chunks = rows // chunk
    big = pl.BlockSpec((rows, dk), lambda h: (0, h))
    gate = pl.BlockSpec((1, levels, rows), lambda h: (h, 0, 0))
    local = pl.BlockSpec((1, chunks, dk, dk), lambda h: (h, 0, 0, 0))
    single = pl.BlockSpec((1, dk, dk), lambda h: (h, 0, 0))
    stacked = pl.BlockSpec((levels - 1, 1, dk, dk), lambda h: (0, h, 0, 0))
    shape = jax.ShapeDtypeStruct
    params = pltpu.CompilerParams(vmem_limit_bytes=VMEM_LIMIT)
    before, after, state, adjoints = pl.pallas_call(
        functools.partial(states_kernel, scaling, chunk),
        grid=(heads,),
        in_specs=[big, big, big, big, gate],
        out_specs=[local, local, single, stacked],
        out_shape=[
            shape((heads, chunks, dk, dk), BF16),
            shape((heads, chunks, dk, dk), BF16),
            shape((heads, dk, dk), F32),
            shape((levels - 1, heads, dk, dk), F32),
        ],
        compiler_params=params,
        name="states",
    )(queries, key_vectors, values, out_grad, level_logits)
    level_states, carried = exchange(state, adjoints)
    grad_q, grad_k, grad_v, level_grad, logit_cot = pl.pallas_call(
        functools.partial(grads_kernel, scaling, chunk),
        grid=(heads,),
        in_specs=[big, big, big, big, gate, local, local, stacked, single],
        out_specs=[big, big, big, gate, gate],
        out_shape=[
            shape((rows, width), BF16),
            shape((rows, width), BF16),
            shape((rows, width), BF16),
            shape((heads, levels, rows), F32),
            shape((heads, levels, rows), BF16),
        ],
        compiler_params=params,
        name="grads",
    )(queries, key_vectors, values, out_grad, level_logits, before, after, level_states, carried)
    hidden_grad = lax.dot_general(
        lax.all_gather(logit_cot.reshape(-1, rows), "head", axis=0, tiled=True),
        level_proj,
        (((0,), (0,)), ((), ())),
        preferred_element_type=F32,
    )
    return grad_q, grad_k, grad_v, level_grad, hidden_grad.astype(BF16)


def solution(mesh):
    in_specs = (
        P("ctx", "head"),
        P("ctx", "head"),
        P("ctx", "head"),
        P("ctx", "head"),
        P("head", None, "ctx"),
        P(None, "head"),
    )
    out_specs = (
        P("ctx", "head"),
        P("ctx", "head"),
        P("ctx", "head"),
        P("head", None, "ctx"),
        P("ctx", "head"),
    )
    return jax.shard_map(body, mesh=mesh, in_specs=in_specs, out_specs=out_specs, check_vma=False)
```

```python
import functools

import jax
import jax.numpy as jnp
from jax import lax
from jax.experimental import pallas as pl
from jax.experimental.pallas import tpu as pltpu
from jax.sharding import PartitionSpec as P

F32 = jnp.float32
BF16 = jnp.bfloat16
VMEM_LIMIT = 56 * 1024 * 1024


def dot(lhs, rhs, contract=((1,), (0,))):
    return lax.dot_general(lhs, rhs, (contract, ((), ())), preferred_element_type=F32)


def softplus(x):
    return jnp.maximum(x, 0.0) + jnp.log1p(jnp.exp(-jnp.abs(x)))


def states_kernel(scaling, chunk, q_ref, k_ref, v_ref, d_ref, logit_ref, sloc_ref, dloc_ref, g_ref, ds_ref):
    rows, dk = q_ref.shape
    levels = logit_ref.shape[1]
    weights = scaling * softplus(logit_ref[0])
    state = jnp.zeros((dk, dk), F32)
    outer = jnp.zeros(((levels - 1) * dk, dk), F32)
    own = []
    for j in range(rows // chunk):
        part = slice(j * chunk, (j + 1) * chunk)
        k_t = k_ref[part, :].T
        q_t = q_ref[part, :].T.astype(F32)
        sloc_ref[0, j] = state.astype(BF16)
        state = state + dot(k_t, v_ref[part, :])
        weighted = jnp.concatenate(
            [(weights[l : l + 1, part] * q_t).astype(BF16) for l in range(levels)], axis=0
        )
        adjoint = dot(weighted, d_ref[part, :])
        own.append(adjoint[:dk])
        outer = outer + adjoint[dk:]
    g_ref[0] = state
    for l in range(levels - 1):
        ds_ref[l, 0] = outer[l * dk : (l + 1) * dk]
    after = jnp.zeros((dk, dk), F32)
    for j in reversed(range(rows // chunk)):
        dloc_ref[0, j] = after.astype(BF16)
        after = after + own[j]


def causal_mask(chunk):
    return lax.broadcasted_iota(jnp.int32, (chunk, chunk), 0) <= lax.broadcasted_iota(
        jnp.int32, (chunk, chunk), 1
    )


def query_kernel(
    scaling, chunk, q_ref, k_ref, v_ref, d_ref, logit_ref, sloc_ref, s_ref, gq_ref, lg_ref, cot_ref
):
    rows, dk = q_ref.shape
    levels = logit_ref.shape[1]
    logits = logit_ref[0]
    gates = softplus(logits)
    weights = scaling * gates
    gate_slope = jax.nn.sigmoid(logits)
    slope = [gate_slope[l : l + 1] * (scaling if l else 1.0 / gates[0:1]) for l in range(levels)]
    outer_states = jnp.concatenate([s_ref[l, 0] for l in range(levels - 1)], axis=0)
    causal = causal_mask(chunk)
    for j in range(rows // chunk):
        part = slice(j * chunk, (j + 1) * chunk)
        q_t, k_t, d_t = q_ref[part, :].T, k_ref[part, :].T, d_ref[part, :].T
        w0 = weights[0:1, part]
        prod_w = (jnp.where(causal, w0, 0.0) * dot(v_ref[part, :], d_t)).astype(BF16)
        q_f = q_t.astype(F32)
        total = dot(k_t, prod_w) + w0 * dot(sloc_ref[0, j], d_t)
        terms = [jnp.sum(q_f * total, axis=0, keepdims=True) * slope[0][:, part]]
        mapped = dot(outer_states, d_t)
        for l in range(1, levels):
            own = mapped[(l - 1) * dk : l * dk]
            total = total + weights[l : l + 1, part] * own
            terms.append(jnp.sum(q_f * own, axis=0, keepdims=True) * slope[l][:, part])
        level_grad = jnp.concatenate(terms, axis=0)
        lg_ref[0, :, part] = level_grad
        cot_ref[0, :, part] = level_grad.astype(BF16)
        gq_ref[part, :] = total.astype(BF16).T


def key_value_kernel(
    scaling, chunk, q_ref, k_ref, v_ref, d_ref, logit_ref, dloc_ref, dg_ref, gk_ref, gv_ref
):
    rows, dk = q_ref.shape
    weights = scaling * softplus(logit_ref[0])
    causal = causal_mask(chunk)
    for j in range(rows // chunk):
        part = slice(j * chunk, (j + 1) * chunk)
        q, k, v, d = q_ref[part, :], k_ref[part, :], v_ref[part, :], d_ref[part, :]
        spread = jnp.where(causal, weights[0:1, part], 0.0)
        score_w = (spread * dot(k, q.T)).astype(BF16)
        prod_w = (spread * dot(v, d.T)).astype(BF16)
        carried = (dloc_ref[0, j].astype(F32) + dg_ref[0]).astype(BF16)
        gk_ref[part, :] = (dot(prod_w, q) + dot(v, carried, ((1,), (1,)))).astype(BF16)
        gv_ref[part, :] = (dot(score_w, d) + dot(k, carried)).astype(BF16)


def exchange_kernel(bits, g_ref, ds_ref, s_ref, dg_ref, *scratch):
    (g_out, g_in, f_out, f_in, c_in, d_out, d_in, d0_out, d0_in, a_out, a_in, t_out, t_in, send_sem, recv_sem) = scratch
    me = lax.axis_index("ctx")
    heads = g_ref.shape[0]
    half = heads // 2
    core = me % 2
    mine, other = pl.ds(core * half, half), pl.ds((1 - core) * half, half)
    peers = [me + (1 << b) - 2 * (1 << b) * ((me // (1 << b)) % 2) for b in range(bits)]
    upper = [((me // (1 << b)) % 2).astype(F32) for b in range(bits)]

    barrier = pltpu.get_barrier_semaphore()
    for peer in peers:
        pl.semaphore_signal(barrier, inc=1, device_id={"ctx": peer}, device_id_type=pl.DeviceIdType.MESH)

    for b in range(1, bits):
        d_out[b - 1] = (upper[b] * ds_ref[b, other]).astype(BF16)
    g_out[...] = g_ref[...].astype(BF16)
    d0_out[...] = (upper[0] * ds_ref[0]).astype(BF16)
    pl.semaphore_wait(barrier, bits)

    copies = []

    def send(src, dst, b):
        i = len(copies)
        copy = pltpu.make_async_remote_copy(
            src_ref=src, dst_ref=dst, send_sem=send_sem.at[i], recv_sem=recv_sem.at[i],
            device_id={"ctx": peers[b]}, device_id_type=pl.DeviceIdType.MESH,
        )
        copy.start()
        copies.append(copy)
        return copy

    d_copy = send(d_out, d_in, 0)
    g_copy = send(g_out, g_in, 0)
    d0_copy = send(d0_out, d0_in, 0)

    carried = jnp.zeros((half,) + g_ref.shape[1:], F32)

    def send_adjoint(b, carried):
        pair = upper[b] * ds_ref[b, mine] + d_in[b - 1].astype(F32)
        a_out[b - 1] = (carried + pair).astype(BF16)
        return send(a_out.at[b - 1], a_in.at[b - 1], b)

    d_copy.wait_recv()
    a_copy = send_adjoint(bits - 1, carried)
    g_copy.wait_recv()
    block = g_ref[mine] + g_in[mine].astype(F32)
    f_out[0] = block.astype(BF16)
    f_copy = send(f_out.at[0], f_in.at[0], 1)
    s_ref[0] = g_in[...] * upper[0].astype(BF16)

    forwards = []

    def forward_step(b, block, f_copy):
        f_copy.wait_recv()
        if b + 1 < bits:
            block = block + f_in[b - 1].astype(F32)
            f_out[b] = block.astype(BF16)
            f_copy = send(f_out.at[b], f_in.at[b], b + 1)
        forwards.append(send(f_in.at[b - 1], c_in.at[b - 1], 0))
        s_ref[b, mine] = f_in[b - 1] * upper[b].astype(BF16)
        return block, f_copy

    def adjoint_step(b, carried, a_copy):
        a_copy.wait_recv()
        carried = carried + a_in[b - 1].astype(F32)
        if b > 1:
            return carried, send_adjoint(b - 1, carried)
        t_out[...] = carried.astype(BF16)
        return carried, send(t_out, t_in, 0)

    for b in range(1, bits):
        if b + 1 < bits:
            block, f_copy = forward_step(b, block, f_copy)
        carried, a_copy = adjoint_step(bits - b, carried, a_copy)
        if b + 1 == bits:
            block, f_copy = forward_step(b, block, f_copy)
    d0_copy.wait_recv()
    dg_ref[mine] = carried + d0_in[mine].astype(F32)
    a_copy.wait_recv()
    dg_ref[other] = t_in[...].astype(F32) + d0_in[other].astype(F32)
    for b in range(1, bits):
        forwards[b - 1].wait_recv()
        s_ref[b, other] = c_in[b - 1] * upper[b].astype(BF16)
    for copy in copies:
        copy.wait_send()


def exchange(state, adjoints):
    heads, dk, _ = state.shape
    bits = adjoints.shape[0]
    half = heads // 2
    whole, parts, one = (heads, dk, dk), (bits - 1, half, dk, dk), (half, dk, dk)
    shapes = [whole, whole, parts, parts, parts, parts, parts, whole, whole, parts, parts, one, one]
    count = 4 + 3 * (bits - 1)
    return pl.pallas_call(
        functools.partial(exchange_kernel, bits),
        in_specs=[pl.BlockSpec(memory_space=pltpu.VMEM)] * 2,
        out_specs=[pl.BlockSpec(memory_space=pltpu.VMEM)] * 2,
        out_shape=[
            jax.ShapeDtypeStruct((bits, heads, dk, dk), BF16),
            jax.ShapeDtypeStruct((heads, dk, dk), F32),
        ],
        scratch_shapes=[pltpu.VMEM(s, BF16) for s in shapes]
        + [pltpu.SemaphoreType.DMA((count,)), pltpu.SemaphoreType.DMA((count,))],
        compiler_params=pltpu.CompilerParams(
            collective_id=0, has_side_effects=True, vmem_limit_bytes=VMEM_LIMIT
        ),
        name="exchange",
    )(state, adjoints)


def body(queries, key_vectors, values, out_grad, level_logits, level_proj):
    rows, width = queries.shape
    heads, levels, _ = level_logits.shape
    dk = width // heads
    scaling = float(dk * rows * lax.axis_size("ctx")) ** (-0.5)
    chunk = min(256, rows)
    chunks = rows // chunk
    big = pl.BlockSpec((rows, dk), lambda h: (0, h))
    gate = pl.BlockSpec((1, levels, rows), lambda h: (h, 0, 0))
    local = pl.BlockSpec((1, chunks, dk, dk), lambda h: (h, 0, 0, 0))
    single = pl.BlockSpec((1, dk, dk), lambda h: (h, 0, 0))
    stacked = pl.BlockSpec((levels - 1, 1, dk, dk), lambda h: (0, h, 0, 0))
    shape = jax.ShapeDtypeStruct
    params = pltpu.CompilerParams(vmem_limit_bytes=VMEM_LIMIT)
    before, after, state, adjoints = pl.pallas_call(
        functools.partial(states_kernel, scaling, chunk),
        grid=(heads,),
        in_specs=[big, big, big, big, gate],
        out_specs=[local, local, single, stacked],
        out_shape=[
            shape((heads, chunks, dk, dk), BF16),
            shape((heads, chunks, dk, dk), BF16),
            shape((heads, dk, dk), F32),
            shape((levels - 1, heads, dk, dk), F32),
        ],
        compiler_params=params,
        name="states",
    )(queries, key_vectors, values, out_grad, level_logits)
    level_states, carried = exchange(state, adjoints)
    wide = shape((rows, width), BF16)
    grad_q, level_grad, logit_cot = pl.pallas_call(
        functools.partial(query_kernel, scaling, chunk),
        grid=(heads,),
        in_specs=[big, big, big, big, gate, local, stacked],
        out_specs=[big, gate, gate],
        out_shape=[wide, shape((heads, levels, rows), F32), shape((heads, levels, rows), BF16)],
        compiler_params=params,
        name="query_grads",
    )(queries, key_vectors, values, out_grad, level_logits, before, level_states)
    own_cot = logit_cot.reshape(heads * levels, rows)
    slices = lax.axis_size("head")
    gathered = [own_cot] + [
        lax.ppermute(own_cot, "head", [(i, (i - hop) % slices) for i in range(slices)])
        for hop in range(1, slices)
    ]
    grad_k, grad_v = pl.pallas_call(
        functools.partial(key_value_kernel, scaling, chunk),
        grid=(heads,),
        in_specs=[big, big, big, big, gate, local, single],
        out_specs=[big, big],
        out_shape=[wide, wide],
        compiler_params=params,
        cost_estimate=pl.CostEstimate(
            flops=2 * rows * width * (4 * chunk + 2 * dk), bytes_accessed=12 * rows * width, transcendentals=0
        ),
        name="key_value_grads",
    )(queries, key_vectors, values, out_grad, level_logits, after, carried)
    turned = lax.dynamic_slice_in_dim(
        jnp.concatenate([level_proj, level_proj], axis=0),
        lax.axis_index("head") * heads * levels, level_proj.shape[0], 0,
    )
    hidden_grad = lax.dot_general(
        jnp.concatenate(gathered, axis=0), turned, (((0,), (0,)), ((), ())), preferred_element_type=F32
    )
    return grad_q, grad_k, grad_v, level_grad, hidden_grad.astype(BF16)


def solution(mesh):
    in_specs = (
        P("ctx", "head"),
        P("ctx", "head"),
        P("ctx", "head"),
        P("ctx", "head"),
        P("head", None, "ctx"),
        P(None, "head"),
    )
    out_specs = (
        P("ctx", "head"),
        P("ctx", "head"),
        P("ctx", "head"),
        P("head", None, "ctx"),
        P("ctx", "head"),
    )
    return jax.shard_map(body, mesh=mesh, in_specs=in_specs, out_specs=out_specs, check_vma=False)
```
